128 devices in a mesh: gx: 64 (over x_hi, y, z, core), gy: 2 (over x_lo).
Axes of the slice: x: 4 (x_hi: 2, x_lo: 2; x = x_hi * 2 + x_lo), y: 4, z: 4, core: 2. Of those that a mesh axis runs over, the one named last changes fastest.
Arguments:
- raw_samples: bfloat16 [2048, 131072], P('gx', 'gy'), may hold values from -6 to 6
- delays: int32 [2048], P('gx'), may hold values from 0 to 2047
- grid_slot: int32 [2048], replicated, may hold values from 0 to 2047, each once
Outputs:
- intensity: bfloat16 [1024, 4, 16384], P('gx', 'gy')
The draws below stay inside these ranges and needn't reach their ends.
Inputs may be any that keep to these rules, and one draw needn't show every extreme that they name: `grid_slot`: each feed has its own slot.
All inputs are finite; a program needn't handle non-finite values.
Results may differ from the reference program's by a relative error of at most 0.0068.
Values may be sent and summed in bfloat16 or wider, within the bound.
No kernel may reach another device: no remote copies, remote signals or barrier semaphores. Data moves between devices by JAX's collectives and lax.ppermute only.
A program may use at most 128 MiB of HBM per device.

```python
import math
import jax
import jax.numpy as jnp
from jax import lax

CHAN = 1024
EW = 4
NS = 256
UP = 16
POLS = 2
PTAPS = 4
UTAPS = 4
NFFT = 2048
NSPAD = 512
BEAMS = 1024
FEEDS = 2048
NFR = 64


def place_ends(values, stream_key, low, largest):
    place = [jax.random.randint(jax.random.fold_in(stream_key, axis), (), 0, length) for axis, length in enumerate(values.shape)]
    longest = values.shape.index(max(values.shape))
    neighbour = place[:longest] + [(place[longest] + 1) % values.shape[longest]] + place[longest + 1:]
    return values.at[tuple(place)].set(low).at[tuple(neighbour)].set(largest)


def block_levels(rng, extent, split, smallest, high):
    gain = 1.0
    for dim, blocks in split:
        heights = jax.random.uniform(jax.random.fold_in(jax.random.fold_in(rng, 6), dim), (blocks,), jnp.float32, smallest / len(split), high / len(split))
        gain = gain * jnp.repeat(jnp.exp(heights), extent[dim] // blocks).reshape((-1,) + (1,) * (len(extent) - 1 - dim))
    return gain


def bell_draw(own_key, shape, scale, most, cuts=(), kind=jnp.bfloat16):
    result = jax.random.normal(own_key, shape, jnp.float32) * scale
    if len(cuts) > 0:
        result = block_levels(own_key, shape, cuts, -0.22, 0.18) * result
    return jnp.clip(result, min=-most, max=most).astype(kind)


def setup_inputs(seed: int = 0) -> dict:
    streams_of = jax.random.split(jax.random.key(seed), 4)
    return {
        "raw_samples": bell_draw(streams_of[0], (FEEDS, NFR * NFFT), 1.0, 6.0, ((0, 64), (1, 2))),
        "delays": place_ends(jax.random.randint(streams_of[1], (FEEDS,), 0, NFFT), jax.random.fold_in(streams_of[1], 1), 0, NFFT - 1).astype(jnp.int32),
        "grid_slot": jax.random.permutation(streams_of[2], FEEDS).astype(jnp.int32),
    }


def taper(tap_count, seg_length):
    total_len = tap_count * seg_length
    places = jnp.arange(total_len, dtype=jnp.float32)
    centre = (places - 0.5 * total_len + 0.5) / seg_length
    hann_part = 0.5 - 0.5 * jnp.cos(2.0 * math.pi * (places + 0.5) / total_len)
    return (jnp.sinc(centre) * hann_part).reshape(tap_count, seg_length)

def dft_table():
    rows = jnp.arange(NFFT, dtype=jnp.int32)
    cols = jnp.arange(CHAN, dtype=jnp.int32)
    phase_index = rows[:, None] * cols[None, :] % NFFT
    phases = phase_index.astype(jnp.float32) * (2.0 * math.pi / NFFT)
    norm_scale = 1.0 / math.sqrt(NFFT)
    return jnp.concatenate([jnp.cos(phases) * norm_scale, -jnp.sin(phases) * norm_scale], axis=1).astype(jnp.bfloat16)

def beam_table():
    slots = jnp.arange(BEAMS, dtype=jnp.int32)
    cyl_pos = slots // NS
    row_pos = slots % NS
    phase_index = (cyl_pos[None, :] * cyl_pos[:, None] * (NSPAD // EW) + row_pos[None, :] * row_pos[:, None]) % NSPAD
    phases = phase_index.astype(jnp.float32) * (2.0 * math.pi / NSPAD)
    norm_scale = 1.0 / math.sqrt(BEAMS)
    cosine = jnp.cos(phases) * norm_scale
    sine_part = jnp.sin(phases) * norm_scale
    upper = jnp.concatenate([cosine, sine_part], axis=1)
    lower = jnp.concatenate([-sine_part, cosine], axis=1)
    return jnp.concatenate([upper, lower], axis=0).astype(jnp.bfloat16)

def upchannel_table():
    fir_taper = taper(UTAPS, UP)
    steps_q = jnp.arange(UP, dtype=jnp.int32)
    phase_index = steps_q[:, None] * steps_q[None, :] % UP
    phases = phase_index.astype(jnp.float32) * (2.0 * math.pi / UP)
    cosine = fir_taper[:, :, None] * jnp.cos(phases)[None]
    sine_part = fir_taper[:, :, None] * jnp.sin(phases)[None]
    from_real = jnp.stack([cosine, -sine_part], axis=-1)
    from_imag = jnp.stack([sine_part, cosine], axis=-1)
    return jnp.stack([from_real, from_imag], axis=2).astype(jnp.bfloat16)

def filter_bank(extended, frame_count):
    weights = taper(PTAPS, NFFT)
    accum = jnp.zeros((extended.shape[0], frame_count, NFFT), jnp.float32)
    for tap in range(PTAPS):
        accum = accum + extended[:, tap:tap + frame_count].astype(jnp.float32) * weights[tap]
    return accum.astype(jnp.bfloat16)

def phase_voltages(spectra, delays):
    cols = jnp.arange(CHAN, dtype=jnp.int32)
    phase_index = delays[:, None] * cols[None, :] % NFFT
    phases = phase_index.astype(jnp.float32) * (2.0 * math.pi / NFFT)
    cosine = jnp.cos(phases)[:, None, :]
    sine_part = jnp.sin(phases)[:, None, :]
    real_part = spectra[..., :CHAN]
    imag_part = spectra[..., CHAN:]
    rot_real = real_part * cosine + imag_part * sine_part
    rot_imag = imag_part * cosine - real_part * sine_part
    return jnp.stack([rot_real, rot_imag], axis=2).astype(jnp.bfloat16)

def form_beams(voltages, feed_at, weights):
    chan_count = voltages.shape[0]
    frame_count = voltages.shape[1]
    slot_feeds = feed_at.reshape(POLS, BEAMS)
    col_index = (jnp.arange(2, dtype=jnp.int32)[None, :, None] * FEEDS + slot_feeds[:, None, :]).reshape(-1)
    flattened = voltages.reshape(chan_count * frame_count, 2 * FEEDS)
    picked = jnp.take(flattened, col_index, axis=1).reshape(chan_count * frame_count * POLS, 2 * BEAMS)
    formed = jnp.dot(picked, weights, preferred_element_type=jnp.float32).astype(jnp.bfloat16)
    return formed.reshape(chan_count, frame_count, POLS, 2, BEAMS)

def upchannel(formed, weights):
    chan_count = formed.shape[0]
    block_count = formed.shape[1] // UP
    leading = jnp.zeros((chan_count, (UTAPS - 1) * UP, POLS, 2, BEAMS), jnp.bfloat16)
    extended = jnp.concatenate([leading, formed], axis=1)
    blocks = extended.reshape(chan_count, UTAPS - 1 + block_count, UP, POLS, 2, BEAMS)
    windows = jnp.stack([blocks[:, tap:tap + block_count] for tap in range(UTAPS)], axis=2)
    subbands = jnp.einsum('cnpqsxb,pqxry->bncrsy', windows.astype(jnp.float32), weights.astype(jnp.float32))
    return (lax.optimization_barrier(jnp.sum(subbands * subbands, axis=(4, 5))) / UP).astype(jnp.bfloat16)

def reference(raw_samples, delays, grid_slot):
    frame_count = raw_samples.shape[1] // NFFT
    frames = raw_samples.reshape(FEEDS, frame_count, NFFT)
    extended = jnp.concatenate([jnp.zeros((FEEDS, PTAPS - 1, NFFT), jnp.bfloat16), frames], axis=1)
    filtered = filter_bank(extended, frame_count)
    spectra = jnp.dot(filtered.reshape(FEEDS * frame_count, NFFT), dft_table(), preferred_element_type=jnp.float32)
    voltages = phase_voltages(spectra.reshape(FEEDS, frame_count, 2 * CHAN), delays)
    turned = jnp.transpose(voltages, (3, 1, 2, 0))
    feed_at = jnp.argsort(grid_slot).astype(jnp.int32)
    beam_weights = beam_table()
    sub_weights = upchannel_table()
    groups = turned.reshape(CHAN // 8, 8, frame_count, 2, FEEDS)

    def per_block(group):
        return upchannel(form_beams(group, feed_at, beam_weights), sub_weights)
    stacked = lax.map(per_block, groups)
    stacked = jnp.transpose(stacked, (1, 2, 0, 3, 4))
    return stacked.reshape(BEAMS, frame_count // UP, CHAN * UP)
```

```python
import functools
import math

import jax
import jax.numpy as jnp
import ml_dtypes
import numpy as np
from jax import lax
from jax.experimental import pallas as pl
from jax.experimental.pallas import tpu as pltpu
from jax.sharding import PartitionSpec as P

CHAN = 1024
EW = 4
NS = 256
UP = 16
POLS = 2
PTAPS = 4
UTAPS = 4
NFFT = 2048
NSPAD = 512
BEAMS = 1024
FEEDS = 2048

LANES = 128
PEERS = 128
CPD = CHAN // PEERS
PPG = 2 * LANES // CPD
SPANS = CHAN // (2 * LANES)
FLOC = 32
HALF = 16
BOTH = ("gx", "gy")
VMEM = 56 * 1024 * 1024


def taper(tap_count, seg_length):
    total_len = tap_count * seg_length
    places = np.arange(total_len, dtype=np.float64)
    centre = (places - 0.5 * total_len + 0.5) / seg_length
    hann_part = 0.5 - 0.5 * np.cos(2.0 * math.pi * (places + 0.5) / total_len)
    return (np.sinc(centre) * hann_part).reshape(tap_count, seg_length).astype(np.float32)


def dft_table():
    rows = np.arange(NFFT // 2)
    cols = np.arange(CHAN).reshape(SPANS, LANES, 2).transpose(0, 2, 1)
    phases = (rows[None, None, :, None] * cols[:, :, None, :] % NFFT) * (2.0 * math.pi / NFFT)
    norm_scale = 1.0 / math.sqrt(NFFT)
    both = np.concatenate([np.cos(phases), -np.sin(phases)], axis=3) * norm_scale
    return both.astype(np.float32).astype(ml_dtypes.bfloat16)


def row_table():
    place = np.arange(NS)
    phases = (place[:, None] * place[None, :] % NSPAD) * (2.0 * math.pi / NSPAD)
    norm_scale = 1.0 / math.sqrt(BEAMS)
    both = np.concatenate([np.cos(phases), np.sin(phases)], axis=0) * norm_scale
    return both.astype(np.float32).astype(ml_dtypes.bfloat16)


def sub_table():
    fir = taper(UTAPS, UP)
    q = np.arange(UP)
    phases = (q[:, None] * q[None, :] % UP) * (2.0 * math.pi / UP)
    cosine = fir[:, :, None] * np.cos(phases).astype(np.float32)[None]
    sine = fir[:, :, None] * np.sin(phases).astype(np.float32)[None]
    table = np.zeros((UTAPS, 2, UP, 2, CPD // 2, 2, CPD, UP), np.float32)
    for k in range(CPD):
        table[:, 0, :, k % 2, k // 2, 0, k, :] = cosine
        table[:, 0, :, k % 2, k // 2, 1, k, :] = -sine
        table[:, 1, :, k % 2, k // 2, 0, k, :] = sine
        table[:, 1, :, k % 2, k // 2, 1, k, :] = cosine
    table = table.reshape(UTAPS, 2, PPG, CPD // 2, 2 * LANES)
    return np.concatenate([table, table], axis=2).astype(ml_dtypes.bfloat16)


def front_kernel(late, raw_ref, halo_ref, w_ref, tab_ref, cos_ref, sin_ref, base_ref, prev_ref, out_ref, *scratch):
    del prev_ref
    ext_ref, x_ref, t_ref, o_ref, raw_sems, tab_sems, out_sems = scratch
    lead = (PTAPS - 1) * NFFT
    part = 1 if late else 0
    if late:
        copies = [
            pltpu.make_async_copy(
                raw_ref.at[:, pl.ds(HALF * NFFT - lead, HALF * NFFT + lead)], ext_ref, raw_sems.at[0]
            )
        ]
    else:
        copies = [
            pltpu.make_async_copy(halo_ref, ext_ref.at[:, pl.ds(0, lead)], raw_sems.at[0]),
            pltpu.make_async_copy(
                raw_ref.at[:, pl.ds(0, HALF * NFFT)], ext_ref.at[:, pl.ds(lead, HALF * NFFT)], raw_sems.at[1]
            ),
        ]
    tables = [pltpu.make_async_copy(tab_ref.at[s], t_ref.at[s], tab_sems.at[s]) for s in range(SPANS)]
    for copy in copies + tables:
        copy.start()
    for copy in copies:
        copy.wait()

    def tile(step, carry):
        at = pl.multiple_of(step * LANES, LANES)
        half = NFFT // 2
        for h in range(2):
            rows = slice(h * 16, h * 16 + 16)
            totals = []
            for side in range(2):
                weights = [w_ref[p : p + 1, pl.ds(at + side * half, LANES)] for p in range(PTAPS)]
                frames = [
                    ext_ref[rows, pl.ds(pl.multiple_of(at + side * half + m * NFFT, LANES), LANES)].astype(jnp.float32)
                    for m in range(HALF + PTAPS - 1)
                ]
                sums = []
                for m in range(HALF):
                    total = frames[m] * weights[0]
                    for p in range(1, PTAPS):
                        total = total + frames[m + p] * weights[p]
                    sums.append(total)
                totals.append(sums)
            for m in range(HALF):
                place = pl.ds(h * 256 + m * 16, 16)
                x_ref[0, place, pl.ds(at, LANES)] = (totals[0][m] + totals[1][m]).astype(jnp.bfloat16)
                x_ref[1, place, pl.ds(at, LANES)] = (totals[0][m] - totals[1][m]).astype(jnp.bfloat16)
        return carry

    lax.fori_loop(0, NFFT // 2 // LANES, tile, 0)

    block = lax.broadcasted_iota(jnp.int32, (16, LANES), 1) // (LANES // PPG)
    bits = [(block // (1 << t)) % 2 == 1 for t in range(5)]
    outs = []
    for s in range(SPANS):
        tables[s].wait()
        spectra = [jnp.dot(x_ref[odd], t_ref[s, odd], preferred_element_type=jnp.float32) for odd in range(2)]
        for h in range(2):
            rows = slice(h * 16, h * 16 + 16)
            cl, sl = cos_ref[rows, :], sin_ref[rows, :]
            parts = [[None] * PPG, [None] * PPG]
            for odd in range(2):
                at = s * 2 + odd
                ca, sa = base_ref[rows, at : at + 1], base_ref[rows, 8 + at : 9 + at]
                cosine, sine = ca * cl - sa * sl, sa * cl + ca * sl
                for m in range(HALF):
                    i = m * 2 + odd
                    row = h * 256 + m * 16
                    real = spectra[odd][row : row + 16, :LANES]
                    imag = spectra[odd][row : row + 16, LANES:]
                    turned = (real * cosine + imag * sine, imag * cosine - real * sine)
                    for x in range(2):
                        value = pltpu.roll(turned[x], i * (LANES // PPG), 1) if i else turned[x]
                        parts[x][i] = value.astype(jnp.bfloat16)
            for x in range(2):
                held = parts[x]
                for t in range(5):
                    held = [jnp.where(bits[t], held[(i + (1 << t)) % PPG], held[i]) for i in range(PPG)]
                for p in range(PPG):
                    o_ref[s, p, x, rows, :] = held[(PPG - p) % PPG]
        copy = pltpu.make_async_copy(o_ref.at[s], out_ref.at[pl.ds(s * PPG, PPG), part], out_sems.at[s])
        copy.start()
        outs.append(copy)
    for copy in outs:
        copy.wait()


def front(late, raw, halo, weights, table, cosine, sine, base, prev):
    wide = (HALF + PTAPS - 1) * NFFT
    whole = pl.BlockSpec(memory_space=pltpu.VMEM)
    there = pl.BlockSpec(memory_space=pl.ANY)
    return pl.pallas_call(
        functools.partial(front_kernel, late),
        in_specs=[there, there, whole, there, whole, whole, whole, there],
        out_specs=there,
        out_shape=jax.ShapeDtypeStruct((PEERS, 2, 2, FLOC, LANES), jnp.bfloat16),
        scratch_shapes=[
            pltpu.VMEM((FLOC, wide), jnp.bfloat16),
            pltpu.VMEM((2, FLOC * HALF, NFFT // 2), jnp.bfloat16),
            pltpu.VMEM((SPANS, 2, NFFT // 2, 2 * LANES), jnp.bfloat16),
            pltpu.VMEM((SPANS, PPG, 2, FLOC, LANES), jnp.bfloat16),
            pltpu.SemaphoreType.DMA((2,)),
            pltpu.SemaphoreType.DMA((SPANS,)),
            pltpu.SemaphoreType.DMA((SPANS,)),
        ],
        input_output_aliases={} if late else {7: 0},
        compiler_params=pltpu.CompilerParams(vmem_limit_bytes=VMEM),
        cost_estimate=pl.CostEstimate(flops=2 * 512 * 1024 * 2048, bytes_accessed=9 << 20, transcendentals=0),
        name="front",
    )(raw, halo, weights, table, cosine, sine, base, prev)


def back_kernel(volt_ref, slot_ref, row_ref, table_ref, out_ref, place_ref, v_ref, vs_ref, beam_ref):
    step = pl.program_id(0)
    wide = 2 * LANES
    for x in range(2):
        v_ref[:, x * LANES : (x + 1) * LANES] = volt_ref[:, 0, 0, x].reshape(FEEDS, LANES)

    @pl.when(step == 0)
    def _():
        slots = slot_ref[...]
        for r in range(FEEDS // NS):
            row = lax.broadcasted_iota(jnp.int32, (NS, FEEDS), 0) + r * NS
            place_ref[r * NS : (r + 1) * NS, :] = jnp.where(row == slots, 1.0, 0.0).astype(jnp.bfloat16)

    for at in range(0, FEEDS, BEAMS):
        placed = jnp.dot(place_ref[at : at + BEAMS, :], v_ref[...], preferred_element_type=jnp.float32)
        vs_ref[at : at + BEAMS, :] = placed.astype(jnp.bfloat16)

    for pol in range(POLS):
        parts = []
        for c in range(EW):
            at = (pol * EW + c) * NS
            both = jnp.dot(row_ref[...], vs_ref[at : at + NS, :], preferred_element_type=jnp.float32)
            cosine, sine = both[:NS], both[NS:]
            parts.append((cosine[:, :LANES] - sine[:, LANES:], cosine[:, LANES:] + sine[:, :LANES]))
        (r0, i0), (r1, i1), (r2, i2), (r3, i3) = parts
        ar, ai, br, bi = r0 + r2, i0 + i2, r0 - r2, i0 - i2
        cr, ci, dr, di = r1 + r3, i1 + i3, r1 - r3, i1 - i3
        formed = [(ar + cr, ai + ci), (br - di, bi + dr), (ar - cr, ai - ci), (br + di, bi - dr)]
        for e in range(EW):
            for x in range(2):
                beam_ref[step, pol, e * NS : (e + 1) * NS, x * LANES : (x + 1) * LANES] = formed[e][x].astype(
                    jnp.bfloat16
                )

    for n in range(4):

        @pl.when(step == n)
        def _(n=n):
            for at in range(0, BEAMS, NS):
                total = None
                for pol in range(POLS):
                    bands = None
                    for j in range(n + 1):
                        tap = (3 - n + j) * wide
                        part = jnp.dot(
                            beam_ref[j, pol, at : at + NS, :],
                            table_ref[tap : tap + wide, :],
                            preferred_element_type=jnp.float32,
                        )
                        bands = part if bands is None else bands + part
                    power = bands * bands
                    total = power if total is None else total + power
                value = (total[:, :LANES] + total[:, LANES:]) * (1.0 / UP)
                out_ref[at // 16 : at // 16 + NS // 16, 0, 0] = value.reshape(NS // 16, 16, LANES).astype(jnp.bfloat16)


def back(volt, slots, rows, table):
    return pl.pallas_call(
        back_kernel,
        grid=(4,),
        in_specs=[
            pl.BlockSpec((PEERS // 2, 1, 1, 2, FLOC, LANES), lambda j: (0, j // 2, j % 2, 0, 0, 0)),
            pl.BlockSpec((1, FEEDS), lambda j: (0, 0)),
            pl.BlockSpec((2 * NS, NS), lambda j: (0, 0)),
            pl.BlockSpec((4 * 2 * LANES, 2 * LANES), lambda j: (0, 0)),
        ],
        out_specs=pl.BlockSpec((BEAMS // 16, 1, 1, 16, LANES), lambda j: (0, j // 2, j % 2, 0, 0)),
        out_shape=jax.ShapeDtypeStruct((BEAMS // 16, 2, 2, 16, LANES), jnp.bfloat16),
        scratch_shapes=[
            pltpu.VMEM((FEEDS, FEEDS), jnp.bfloat16),
            pltpu.VMEM((FEEDS, 2 * LANES), jnp.bfloat16),
            pltpu.VMEM((FEEDS, 2 * LANES), jnp.bfloat16),
            pltpu.VMEM((4, POLS, BEAMS, 2 * LANES), jnp.bfloat16),
        ],
        compiler_params=pltpu.CompilerParams(vmem_limit_bytes=VMEM),
        cost_estimate=pl.CostEstimate(flops=14 << 30, bytes_accessed=6 << 20, transcendentals=0),
        name="back",
    )(volt.reshape(PEERS // 2, 2, 2, 2, FLOC, LANES), slots, rows, table)


def body(raw_samples, delays, grid_slot):
    rim = raw_samples[:, raw_samples.shape[1] - (PTAPS - 1) * NFFT :]
    halo = lax.ppermute(rim, "gy", [(0, 1)])
    steps = jnp.concatenate([2 * jnp.arange(LANES), 256 * (jnp.arange(8) // 2) + jnp.arange(8) % 2]).astype(jnp.int32)
    phases = (delays[:, None] * steps[None, :] % NFFT).astype(jnp.float32) * (2.0 * math.pi / NFFT)
    cosine, sine = jnp.cos(phases), jnp.sin(phases)
    base = jnp.concatenate([cosine[:, LANES:], sine[:, LANES:]], axis=1)
    cosine, sine = cosine[:, :LANES], sine[:, :LANES]
    weights = jnp.asarray(taper(PTAPS, NFFT))
    table = jnp.asarray(dft_table())
    rows = jnp.asarray(row_table())
    me = lax.axis_index(BOTH)
    sub = lax.dynamic_slice_in_dim(jnp.asarray(sub_table()), PPG - me % PPG, PPG, axis=2)
    sub = sub.reshape(UTAPS * 2 * LANES, 2 * LANES)

    volt = front(True, raw_samples, rim, weights, table, cosine, sine, base, rim)
    volt = front(False, raw_samples, halo, weights, table, cosine, sine, base, volt)
    volt = lax.all_to_all(volt, BOTH, 0, 0, tiled=True)
    intens = back(volt, grid_slot.reshape(1, FEEDS), rows, sub).reshape(PEERS, 2, 16, LANES)
    intens = lax.all_to_all(intens, BOTH, 0, 0, tiled=True)
    return jnp.transpose(intens, (2, 1, 0, 3)).reshape(16, 2, CHAN * UP)


def solution(mesh):
    return jax.shard_map(
        body,
        mesh=mesh,
        in_specs=(P("gx", "gy"), P("gx"), P()),
        out_specs=P("gx", "gy", None),
        check_vma=False,
    )
```

```python
import functools
import math

import jax
import jax.numpy as jnp
import ml_dtypes
import numpy as np
from jax import lax
from jax.experimental import pallas as pl
from jax.experimental.pallas import tpu as pltpu
from jax.sharding import PartitionSpec as P

CHAN = 1024
EW = 4
NS = 256
UP = 16
POLS = 2
PTAPS = 4
UTAPS = 4
NFFT = 2048
NSPAD = 512
BEAMS = 1024
FEEDS = 2048

LANES = 128
PEERS = 128
CPD = CHAN // PEERS
PPG = 2 * LANES // CPD
SPANS = CHAN // (2 * LANES)
FLOC = 32
HALF = 16
BOTH = ("gx", "gy")
MIB = 1024 * 1024
SPARE = 16


def taper(tap_count, seg_length):
    total_len = tap_count * seg_length
    places = np.arange(total_len, dtype=np.float64)
    centre = (places - 0.5 * total_len + 0.5) / seg_length
    hann_part = 0.5 - 0.5 * np.cos(2.0 * math.pi * (places + 0.5) / total_len)
    return (np.sinc(centre) * hann_part).reshape(tap_count, seg_length).astype(np.float32)


def dft_table():
    rows = np.arange(NFFT // 2)
    cols = np.arange(CHAN).reshape(SPANS, LANES, 2).transpose(0, 2, 1)
    phases = (rows[None, None, :, None] * cols[:, :, None, :] % NFFT) * (2.0 * math.pi / NFFT)
    norm_scale = 1.0 / math.sqrt(NFFT)
    both = np.concatenate([np.cos(phases), -np.sin(phases)], axis=3) * norm_scale
    return both.astype(np.float32).astype(ml_dtypes.bfloat16)


def row_table():
    place = np.arange(NS)
    phases = (place[:, None] * place[None, :] % NSPAD) * (2.0 * math.pi / NSPAD)
    norm_scale = 1.0 / math.sqrt(BEAMS)
    both = np.concatenate([np.cos(phases), np.sin(phases)], axis=0) * norm_scale
    return both.astype(np.float32).astype(ml_dtypes.bfloat16)


def sub_table():
    fir = taper(UTAPS, UP)
    q = np.arange(UP)
    phases = (q[:, None] * q[None, :] % UP) * (2.0 * math.pi / UP)
    cosine = fir[:, :, None] * np.cos(phases).astype(np.float32)[None]
    sine = fir[:, :, None] * np.sin(phases).astype(np.float32)[None]
    table = np.zeros((UTAPS, 2, UP, 2, CPD // 2, 2, CPD, UP), np.float32)
    for k in range(CPD):
        table[:, 0, :, k % 2, k // 2, 0, k, :] = cosine
        table[:, 0, :, k % 2, k // 2, 1, k, :] = -sine
        table[:, 1, :, k % 2, k // 2, 0, k, :] = sine
        table[:, 1, :, k % 2, k // 2, 1, k, :] = cosine
    table = table.reshape(UTAPS, 2, PPG, CPD // 2, 2 * LANES)
    return np.concatenate([table, table], axis=2).astype(ml_dtypes.bfloat16)


def turns(index):
    quarter = (index + NFFT // 8) // (NFFT // 4)
    angle = (index - quarter * (NFFT // 4)).astype(jnp.float32) * (2.0 * math.pi / NFFT)
    sq = angle * angle
    sine = angle * (1.0 + sq * (-1.0 / 6 + sq * (1.0 / 120 + sq * (-1.0 / 5040 + sq * (1.0 / 362880)))))
    cosine = 1.0 + sq * (-1.0 / 2 + sq * (1.0 / 24 + sq * (-1.0 / 720 + sq * (1.0 / 40320 - sq * (1.0 / 3628800)))))
    odd = quarter % 2 == 1
    first, second = jnp.where(odd, -sine, cosine), jnp.where(odd, cosine, sine)
    back = (quarter // 2) % 2 == 1
    return jnp.where(back, -first, first), jnp.where(back, -second, second)


def front_kernel(late, raw_ref, halo_ref, delay_ref, w_ref, tab_ref, out_ref, *scratch):
    ext_ref, x_ref, t_ref, o_ref, cos_ref, sin_ref, raw_sems, tab_sems, out_sems = scratch
    lead = (PTAPS - 1) * NFFT
    if late:
        copies = [
            pltpu.make_async_copy(
                raw_ref.at[:, pl.ds(HALF * NFFT - lead, HALF * NFFT + lead)], ext_ref, raw_sems.at[0]
            )
        ]
    else:
        copies = [
            pltpu.make_async_copy(halo_ref, ext_ref.at[:, pl.ds(0, lead)], raw_sems.at[0]),
            pltpu.make_async_copy(
                raw_ref.at[:, pl.ds(0, HALF * NFFT)], ext_ref.at[:, pl.ds(lead, HALF * NFFT)], raw_sems.at[1]
            ),
        ]
    tables = [pltpu.make_async_copy(tab_ref.at[s], t_ref.at[s], tab_sems.at[s]) for s in range(SPANS)]
    for copy in copies:
        copy.start()

    sub = lax.broadcasted_iota(jnp.int32, (8, LANES), 0)
    lane = lax.broadcasted_iota(jnp.int32, (8, LANES), 1)
    for g in range(FLOC // 8):
        delay = jnp.zeros((8, LANES), jnp.int32)
        for i in range(8):
            delay = jnp.where(sub == i, delay_ref[g * 8 + i], delay)
        for s in range(SPANS):
            for odd in range(2):
                cosine, sine = turns((delay * (2 * LANES * s + odd + 2 * lane)) % NFFT)
                cos_ref[s * 2 + odd, g * 8 : g * 8 + 8, :] = cosine
                sin_ref[s * 2 + odd, g * 8 : g * 8 + 8, :] = sine

    for copy in copies:
        copy.wait()
    for copy in tables:
        copy.start()

    def tile(step, carry):
        at = pl.multiple_of(step * LANES, LANES)
        half = NFFT // 2
        for h in range(2):
            rows = slice(h * 16, h * 16 + 16)
            totals = []
            for side in range(2):
                weights = [w_ref[p : p + 1, pl.ds(at + side * half, LANES)] for p in range(PTAPS)]
                frames = [
                    ext_ref[rows, pl.ds(pl.multiple_of(at + side * half + m * NFFT, LANES), LANES)].astype(jnp.float32)
                    for m in range(HALF + PTAPS - 1)
                ]
                sums = []
                for m in range(HALF):
                    total = frames[m] * weights[0]
                    for p in range(1, PTAPS):
                        total = total + frames[m + p] * weights[p]
                    sums.append(total)
                totals.append(sums)
            for m in range(HALF):
                place = pl.ds(h * 256 + m * 16, 16)
                x_ref[0, place, pl.ds(at, LANES)] = (totals[0][m] + totals[1][m]).astype(jnp.bfloat16)
                x_ref[1, place, pl.ds(at, LANES)] = (totals[0][m] - totals[1][m]).astype(jnp.bfloat16)
        return carry

    lax.fori_loop(0, NFFT // 2 // LANES, tile, 0)

    block = lax.broadcasted_iota(jnp.int32, (16, LANES), 1) // (LANES // PPG)
    bits = [(block // (1 << t)) % 2 == 1 for t in range(5)]
    outs = []
    for s in range(SPANS):
        tables[s].wait()
        spectra = [jnp.dot(x_ref[odd], t_ref[s, odd], preferred_element_type=jnp.float32) for odd in range(2)]
        for h in range(2):
            rows = slice(h * 16, h * 16 + 16)
            parts = [[None] * PPG, [None] * PPG]
            for odd in range(2):
                cosine, sine = cos_ref[s * 2 + odd, rows, :], sin_ref[s * 2 + odd, rows, :]
                for m in range(HALF):
                    i = m * 2 + odd
                    row = h * 256 + m * 16
                    real = spectra[odd][row : row + 16, :LANES]
                    imag = spectra[odd][row : row + 16, LANES:]
                    turned = (real * cosine + imag * sine, imag * cosine - real * sine)
                    for x in range(2):
                        value = pltpu.roll(turned[x], i * (LANES // PPG), 1) if i else turned[x]
                        parts[x][i] = value.astype(jnp.bfloat16)
            for x in range(2):
                held = parts[x]
                for t in range(5):
                    held = [jnp.where(bits[t], held[(i + (1 << t)) % PPG], held[i]) for i in range(PPG)]
                for p in range(PPG):
                    o_ref[s, p, x, rows, :] = held[(PPG - p) % PPG]
        copy = pltpu.make_async_copy(o_ref.at[s], out_ref.at[pl.ds(s * PPG, PPG)], out_sems.at[s])
        copy.start()
        outs.append(copy)
    for copy in outs:
        copy.wait()


def front(late, raw, halo, delays, weights, table):
    wide = (HALF + PTAPS - 1) * NFFT
    there = pl.BlockSpec(memory_space=pl.ANY)
    return pl.pallas_call(
        functools.partial(front_kernel, late),
        in_specs=[
            pl.BlockSpec(memory_space=pltpu.HBM),
            there,
            pl.BlockSpec(memory_space=pltpu.SMEM),
            pl.BlockSpec(memory_space=pltpu.VMEM),
            pl.BlockSpec(memory_space=pltpu.HBM),
        ],
        out_specs=there,
        out_shape=jax.ShapeDtypeStruct((PEERS, 2, FLOC, LANES), jnp.bfloat16),
        scratch_shapes=[
            pltpu.VMEM((FLOC, wide), jnp.bfloat16),
            pltpu.VMEM((2, FLOC * HALF, NFFT // 2), jnp.bfloat16),
            pltpu.VMEM((SPANS, 2, NFFT // 2, 2 * LANES), jnp.bfloat16),
            pltpu.VMEM((SPANS, PPG, 2, FLOC, LANES), jnp.bfloat16),
            pltpu.VMEM((2 * SPANS, FLOC, LANES), jnp.float32),
            pltpu.VMEM((2 * SPANS, FLOC, LANES), jnp.float32),
            pltpu.SemaphoreType.DMA((2,)),
            pltpu.SemaphoreType.DMA((SPANS,)),
            pltpu.SemaphoreType.DMA((SPANS,)),
        ],
        compiler_params=pltpu.CompilerParams(vmem_limit_bytes=(58 if late else 30) * MIB),
        cost_estimate=pl.CostEstimate(flops=2 * 512 * 1024 * 2048, bytes_accessed=9 << 20, transcendentals=0),
        name="front_late" if late else "front_early",
    )(raw, halo, delays, weights, table)


def fetch_volts(volt_ref, v_ref, sems):
    return [
        pltpu.make_async_copy(
            volt_ref.at[:, gy, x], v_ref.at[gy, :, :, pl.ds(x * LANES, LANES)], sems.at[gy * 2 + x]
        )
        for gy in range(2)
        for x in range(2)
    ]


def mark_places(slot_ref, place_ref):
    slots = slot_ref[...]
    for r in range(FEEDS // NS):
        row = lax.broadcasted_iota(jnp.int32, (NS, FEEDS), 0) + r * NS
        place_ref[r * NS : (r + 1) * NS, :] = jnp.where(row == slots, 1.0, 0.0).astype(jnp.bfloat16)


def form_beams(volts, row_ref, place_ref, vs_ref, store):
    for at in range(0, FEEDS, BEAMS):
        placed = jnp.dot(place_ref[at : at + BEAMS, :], volts, preferred_element_type=jnp.float32)
        vs_ref[at : at + BEAMS, :] = placed.astype(jnp.bfloat16)
    for pol in range(POLS):
        parts = []
        for c in range(EW):
            at = (pol * EW + c) * NS
            both = jnp.dot(row_ref[...], vs_ref[at : at + NS, :], preferred_element_type=jnp.float32)
            cosine, sine = both[:NS], both[NS:]
            parts.append((cosine[:, :LANES] - sine[:, LANES:], cosine[:, LANES:] + sine[:, :LANES]))
        (r0, i0), (r1, i1), (r2, i2), (r3, i3) = parts
        ar, ai, br, bi = r0 + r2, i0 + i2, r0 - r2, i0 - i2
        cr, ci, dr, di = r1 + r3, i1 + i3, r1 - r3, i1 - i3
        formed = [(ar + cr, ai + ci), (br - di, bi + dr), (ar - cr, ai - ci), (br + di, bi - dr)]
        for e in range(EW):
            for x in range(2):
                store(pol, e * NS, x * LANES, formed[e][x].astype(jnp.bfloat16))


def late_kernel(volt_ref, slot_ref, row_ref, out_ref, place_ref, v_ref, vs_ref, beam_ref, sems):
    copies = fetch_volts(volt_ref, v_ref, sems)
    for copy in copies:
        copy.start()
    mark_places(slot_ref, place_ref)
    outs = []
    for gy in range(2):
        copies[gy * 2].wait()
        copies[gy * 2 + 1].wait()

        def store(pol, row, lane, value, gy=gy):
            beam_ref[gy, pol, row : row + NS, lane : lane + LANES] = value

        form_beams(v_ref[gy].reshape(FEEDS, 2 * LANES), row_ref, place_ref, vs_ref, store)
        outs.append(pltpu.make_async_copy(beam_ref.at[gy], out_ref.at[gy], sems.at[4 + gy]))
        outs[gy].start()
    for copy in outs:
        copy.wait()


def early_kernel(volt_ref, slot_ref, row_ref, late_ref, table_ref, out_ref, place_ref, v_ref, vs_ref, beam_ref, sems):
    wide = 2 * LANES
    copies = fetch_volts(volt_ref, v_ref, sems)
    for gy in range(2):
        copies.append(
            pltpu.make_async_copy(
                late_ref.at[gy], beam_ref.at[:, :, pl.ds((gy * 2 + 1) * wide, wide)], sems.at[4 + gy]
            )
        )
    for copy in copies:
        copy.start()
    mark_places(slot_ref, place_ref)
    for gy in range(2):
        copies[gy * 2].wait()
        copies[gy * 2 + 1].wait()

        def store(pol, row, lane, value, gy=gy):
            at = gy * 2 * wide + lane
            beam_ref[pol, row : row + NS, at : at + LANES] = value

        form_beams(v_ref[gy].reshape(FEEDS, wide), row_ref, place_ref, vs_ref, store)
        copies[4 + gy].wait()
        for n in range(gy * 2, gy * 2 + 2):
            for at in range(0, BEAMS, NS):
                total = None
                for pol in range(POLS):
                    bands = jnp.dot(
                        beam_ref[pol, at : at + NS, : (n + 1) * wide],
                        table_ref[(3 - n) * wide :, :],
                        preferred_element_type=jnp.float32,
                    )
                    power = bands * bands
                    total = power if total is None else total + power
                value = (total[:, :LANES] + total[:, LANES:]) * (1.0 / UP)
                out_ref[at // 16 : at // 16 + NS // 16, gy, n % 2] = value.reshape(NS // 16, 16, LANES).astype(
                    jnp.bfloat16
                )


def back(volt, slots, rows, *more):
    whole = pl.BlockSpec(memory_space=pltpu.VMEM)
    there = pl.BlockSpec(memory_space=pl.ANY)
    far = pl.BlockSpec(memory_space=pltpu.HBM)
    scratch = [
        pltpu.VMEM((FEEDS, FEEDS), jnp.bfloat16),
        pltpu.VMEM((2, PEERS // 2, FLOC, 2 * LANES), jnp.bfloat16),
        pltpu.VMEM((FEEDS, 2 * LANES), jnp.bfloat16),
    ]
    if more:
        kernel, specs, name = early_kernel, [there, whole, whole, far, whole], "back_early"
        shape, out = (BEAMS // 16, 2, 2, 16, LANES), whole
        scratch += [pltpu.VMEM((POLS, BEAMS, 4 * 2 * LANES), jnp.bfloat16), pltpu.SemaphoreType.DMA((6,))]
    else:
        kernel, specs, name = late_kernel, [there, whole, whole], "back_late"
        shape, out = (SPARE, POLS, BEAMS, 2 * LANES), far
        scratch += [pltpu.VMEM((2, POLS, BEAMS, 2 * LANES), jnp.bfloat16), pltpu.SemaphoreType.DMA((6,))]
    return pl.pallas_call(
        kernel,
        in_specs=specs,
        out_specs=out,
        out_shape=jax.ShapeDtypeStruct(shape, jnp.bfloat16),
        scratch_shapes=scratch,
        compiler_params=pltpu.CompilerParams(vmem_limit_bytes=(48 if more else 40) * MIB),
        cost_estimate=pl.CostEstimate(flops=6 << 30, bytes_accessed=6 << 20, transcendentals=0),
        name=name,
    )(volt.reshape(PEERS // 2, 2, 2, FLOC, LANES), slots, rows, *more)


def body(raw_samples, delays, grid_slot):
    rim = raw_samples[:, raw_samples.shape[1] - (PTAPS - 1) * NFFT :]
    halo = lax.ppermute(rim, "gy", [(0, 1)])
    weights = jnp.asarray(taper(PTAPS, NFFT))
    table = jnp.asarray(dft_table())
    rows = jnp.asarray(row_table())
    slots = grid_slot.reshape(1, FEEDS)
    me = lax.axis_index(BOTH)
    sub = lax.dynamic_slice_in_dim(jnp.asarray(sub_table()), PPG - me % PPG, PPG, axis=2)
    sub = sub.reshape(UTAPS * 2 * LANES, 2 * LANES)

    late = front(True, raw_samples, rim, delays, weights, table)
    late, halo = lax.optimization_barrier((late, halo))
    late = lax.all_to_all(late, BOTH, 0, 0, tiled=True)
    early = front(False, raw_samples, halo, delays, weights, table)
    early, late = lax.optimization_barrier((early, late))
    early = lax.all_to_all(early, BOTH, 0, 0, tiled=True)
    beams = back(late, slots, rows)
    intens = back(early, slots, rows, beams, sub).reshape(PEERS, 2, 16, LANES)
    intens = lax.all_to_all(intens, BOTH, 0, 0, tiled=True)
    return jnp.transpose(intens, (2, 1, 0, 3)).reshape(16, 2, CHAN * UP)


def solution(mesh):
    return jax.shard_map(
        body,
        mesh=mesh,
        in_specs=(P("gx", "gy"), P("gx"), P()),
        out_specs=P("gx", "gy", None),
        check_vma=False,
    )
```

```python
import functools
import math

import jax
import jax.numpy as jnp
import ml_dtypes
import numpy as np
from jax import lax
from jax.experimental import pallas as pl
from jax.experimental.pallas import tpu as pltpu
from jax.sharding import PartitionSpec as P

CHAN = 1024
EW = 4
NS = 256
UP = 16
POLS = 2
PTAPS = 4
UTAPS = 4
NFFT = 2048
NSPAD = 512
BEAMS = 1024
FEEDS = 2048

LANES = 128
PEERS = 128
CPD = CHAN // PEERS
PPG = 2 * LANES // CPD
SPANS = CHAN // (2 * LANES)
FLOC = 32
HALF = 16
BOTH = ("gx", "gy")
MIB = 1024 * 1024
SPARE = 16


def taper(tap_count, seg_length):
    total_len = tap_count * seg_length
    places = np.arange(total_len, dtype=np.float64)
    centre = (places - 0.5 * total_len + 0.5) / seg_length
    hann_part = 0.5 - 0.5 * np.cos(2.0 * math.pi * (places + 0.5) / total_len)
    return (np.sinc(centre) * hann_part).reshape(tap_count, seg_length).astype(np.float32)


def dft_table():
    rows = np.arange(NFFT // 2)
    cols = np.arange(CHAN).reshape(SPANS, LANES, 2).transpose(0, 2, 1)
    phases = (rows[None, None, :, None] * cols[:, :, None, :] % NFFT) * (2.0 * math.pi / NFFT)
    norm_scale = 1.0 / math.sqrt(NFFT)
    both = np.concatenate([np.cos(phases), -np.sin(phases)], axis=3) * norm_scale
    return both.astype(np.float32).astype(ml_dtypes.bfloat16)


def row_table():
    place = np.arange(NS)
    phases = (place[:, None] * place[None, :] % NSPAD) * (2.0 * math.pi / NSPAD)
    norm_scale = 1.0 / math.sqrt(BEAMS)
    both = np.concatenate([np.cos(phases), np.sin(phases)], axis=0) * norm_scale
    return both.astype(np.float32).astype(ml_dtypes.bfloat16)


def sub_table():
    fir = taper(UTAPS, UP)
    q = np.arange(UP)
    phases = (q[:, None] * q[None, :] % UP) * (2.0 * math.pi / UP)
    cosine = fir[:, :, None] * np.cos(phases).astype(np.float32)[None]
    sine = fir[:, :, None] * np.sin(phases).astype(np.float32)[None]
    table = np.zeros((UTAPS, 2, UP, 2, CPD // 2, 2, CPD, UP), np.float32)
    for k in range(CPD):
        table[:, 0, :, k % 2, k // 2, 0, k, :] = cosine
        table[:, 0, :, k % 2, k // 2, 1, k, :] = -sine
        table[:, 1, :, k % 2, k // 2, 0, k, :] = sine
        table[:, 1, :, k % 2, k // 2, 1, k, :] = cosine
    table = table.reshape(UTAPS, 2, PPG, CPD // 2, 2 * LANES)
    return np.concatenate([table, table], axis=2).astype(ml_dtypes.bfloat16)


def turns(index):
    quarter = (index + NFFT // 8) // (NFFT // 4)
    angle = (index - quarter * (NFFT // 4)).astype(jnp.float32) * (2.0 * math.pi / NFFT)
    sq = angle * angle
    sine = angle * (1.0 + sq * (-1.0 / 6 + sq * (1.0 / 120 + sq * (-1.0 / 5040 + sq * (1.0 / 362880)))))
    cosine = 1.0 + sq * (-1.0 / 2 + sq * (1.0 / 24 + sq * (-1.0 / 720 + sq * (1.0 / 40320 - sq * (1.0 / 3628800)))))
    odd = quarter % 2 == 1
    first, second = jnp.where(odd, -sine, cosine), jnp.where(odd, cosine, sine)
    back = (quarter // 2) % 2 == 1
    return jnp.where(back, -first, first), jnp.where(back, -second, second)


def front_kernel(late, raw_ref, halo_ref, delay_ref, w_ref, tab_ref, out_ref, *scratch):
    ext_ref, x_ref, t_ref, o_ref, cos_ref, sin_ref, raw_sems, tab_sems, out_sems = scratch
    lead = (PTAPS - 1) * NFFT
    copies = []
    for h in range(2):
        rows = pl.ds(h * 16, 16)
        if late:
            pairs = [(raw_ref.at[rows, pl.ds(HALF * NFFT - lead, HALF * NFFT + lead)], ext_ref.at[rows, :])]
        else:
            pairs = [
                (raw_ref.at[rows, pl.ds(0, HALF * NFFT)], ext_ref.at[rows, pl.ds(lead, HALF * NFFT)]),
                (halo_ref.at[rows, :], ext_ref.at[rows, pl.ds(0, lead)]),
            ]
        copies.append([pltpu.make_async_copy(src, dst, raw_sems.at[h, i]) for i, (src, dst) in enumerate(pairs)])
    tables = [pltpu.make_async_copy(tab_ref.at[s], t_ref.at[s], tab_sems.at[s]) for s in range(SPANS)]
    for copy in copies[0] + copies[1]:
        copy.start()

    sub = lax.broadcasted_iota(jnp.int32, (8, LANES), 0)
    lane = lax.broadcasted_iota(jnp.int32, (8, LANES), 1)
    for g in range(FLOC // 8):
        delay = jnp.zeros((8, LANES), jnp.int32)
        for i in range(8):
            delay = jnp.where(sub == i, delay_ref[g * 8 + i], delay)
        for s in range(SPANS):
            for odd in range(2):
                cosine, sine = turns((delay * (2 * LANES * s + odd + 2 * lane)) % NFFT)
                cos_ref[s * 2 + odd, g * 8 : g * 8 + 8, :] = cosine
                sin_ref[s * 2 + odd, g * 8 : g * 8 + 8, :] = sine

    def tile(h, step, carry):
        at = pl.multiple_of(step * LANES, LANES)
        half = NFFT // 2
        rows = slice(h * 16, h * 16 + 16)
        totals = []
        for side in range(2):
            weights = [w_ref[p : p + 1, pl.ds(at + side * half, LANES)] for p in range(PTAPS)]
            frames = [
                ext_ref[rows, pl.ds(pl.multiple_of(at + side * half + m * NFFT, LANES), LANES)].astype(jnp.float32)
                for m in range(HALF + PTAPS - 1)
            ]
            sums = []
            for m in range(HALF):
                total = frames[m] * weights[0]
                for p in range(1, PTAPS):
                    total = total + frames[m + p] * weights[p]
                sums.append(total)
            totals.append(sums)
        for m in range(HALF):
            place = pl.ds(h * 256 + m * 16, 16)
            x_ref[0, place, pl.ds(at, LANES)] = (totals[0][m] + totals[1][m]).astype(jnp.bfloat16)
            x_ref[1, place, pl.ds(at, LANES)] = (totals[0][m] - totals[1][m]).astype(jnp.bfloat16)
        return carry

    for h in range(2):
        for copy in copies[h]:
            copy.wait()
        if h == 0:
            for copy in tables:
                copy.start()
        lax.fori_loop(0, NFFT // 2 // LANES, functools.partial(tile, h), 0)

    block = lax.broadcasted_iota(jnp.int32, (16, LANES), 1) // (LANES // PPG)
    bits = [(block // (1 << t)) % 2 == 1 for t in range(5)]
    outs = []
    for s in range(SPANS):
        tables[s].wait()
        spectra = [jnp.dot(x_ref[odd], t_ref[s, odd], preferred_element_type=jnp.float32) for odd in range(2)]
        for h in range(2):
            rows = slice(h * 16, h * 16 + 16)
            parts = [[None] * PPG, [None] * PPG]
            for odd in range(2):
                cosine, sine = cos_ref[s * 2 + odd, rows, :], sin_ref[s * 2 + odd, rows, :]
                for m in range(HALF):
                    i = m * 2 + odd
                    row = h * 256 + m * 16
                    real = spectra[odd][row : row + 16, :LANES]
                    imag = spectra[odd][row : row + 16, LANES:]
                    turned = (real * cosine + imag * sine, imag * cosine - real * sine)
                    for x in range(2):
                        value = pltpu.roll(turned[x], i * (LANES // PPG), 1) if i else turned[x]
                        parts[x][i] = value.astype(jnp.bfloat16)
            for x in range(2):
                held = parts[x]
                for t in range(5):
                    held = [jnp.where(bits[t], held[(i + (1 << t)) % PPG], held[i]) for i in range(PPG)]
                for p in range(PPG):
                    o_ref[s, p, x, rows, :] = held[(PPG - p) % PPG]
        copy = pltpu.make_async_copy(o_ref.at[s], out_ref.at[pl.ds(s * PPG, PPG)], out_sems.at[s])
        copy.start()
        outs.append(copy)
    for copy in outs:
        copy.wait()


def front(late, raw, halo, delays, weights, table):
    wide = (HALF + PTAPS - 1) * NFFT
    there = pl.BlockSpec(memory_space=pl.ANY)
    return pl.pallas_call(
        functools.partial(front_kernel, late),
        in_specs=[
            pl.BlockSpec(memory_space=pltpu.HBM),
            there,
            pl.BlockSpec(memory_space=pltpu.SMEM),
            pl.BlockSpec(memory_space=pltpu.VMEM),
            pl.BlockSpec(memory_space=pltpu.HBM),
        ],
        out_specs=there,
        out_shape=jax.ShapeDtypeStruct((PEERS, 2, FLOC, LANES), jnp.bfloat16),
        scratch_shapes=[
            pltpu.VMEM((FLOC, wide), jnp.bfloat16),
            pltpu.VMEM((2, FLOC * HALF, NFFT // 2), jnp.bfloat16),
            pltpu.VMEM((SPANS, 2, NFFT // 2, 2 * LANES), jnp.bfloat16),
            pltpu.VMEM((SPANS, PPG, 2, FLOC, LANES), jnp.bfloat16),
            pltpu.VMEM((2 * SPANS, FLOC, LANES), jnp.float32),
            pltpu.VMEM((2 * SPANS, FLOC, LANES), jnp.float32),
            pltpu.SemaphoreType.DMA((2, 2)),
            pltpu.SemaphoreType.DMA((SPANS,)),
            pltpu.SemaphoreType.DMA((SPANS,)),
        ],
        compiler_params=pltpu.CompilerParams(vmem_limit_bytes=(58 if late else 30) * MIB),
        cost_estimate=pl.CostEstimate(flops=2 * 512 * 1024 * 2048, bytes_accessed=9 << 20, transcendentals=0),
        name="front_late" if late else "front_early",
    )(raw, halo, delays, weights, table)


def fetch_volts(volt_ref, v_ref, sems):
    return [
        pltpu.make_async_copy(
            volt_ref.at[:, gy, x], v_ref.at[gy, :, :, pl.ds(x * LANES, LANES)], sems.at[gy * 2 + x]
        )
        for gy in range(2)
        for x in range(2)
    ]


def mark_places(slot_ref, place_ref):
    slots = slot_ref[...]
    for r in range(FEEDS // NS):
        row = lax.broadcasted_iota(jnp.int32, (NS, FEEDS), 0) + r * NS
        place_ref[r * NS : (r + 1) * NS, :] = jnp.where(row == slots, 1.0, 0.0).astype(jnp.bfloat16)


def form_beams(volts, row_ref, place_ref, vs_ref, store):
    for at in range(0, FEEDS, BEAMS):
        placed = jnp.dot(place_ref[at : at + BEAMS, :], volts, preferred_element_type=jnp.float32)
        vs_ref[at : at + BEAMS, :] = placed.astype(jnp.bfloat16)
    for pol in range(POLS):
        parts = []
        for c in range(EW):
            at = (pol * EW + c) * NS
            both = jnp.dot(row_ref[...], vs_ref[at : at + NS, :], preferred_element_type=jnp.float32)
            cosine, sine = both[:NS], both[NS:]
            parts.append((cosine[:, :LANES] - sine[:, LANES:], cosine[:, LANES:] + sine[:, :LANES]))
        (r0, i0), (r1, i1), (r2, i2), (r3, i3) = parts
        ar, ai, br, bi = r0 + r2, i0 + i2, r0 - r2, i0 - i2
        cr, ci, dr, di = r1 + r3, i1 + i3, r1 - r3, i1 - i3
        formed = [(ar + cr, ai + ci), (br - di, bi + dr), (ar - cr, ai - ci), (br + di, bi - dr)]
        for e in range(EW):
            for x in range(2):
                store(pol, e * NS, x * LANES, formed[e][x].astype(jnp.bfloat16))


def late_kernel(volt_ref, slot_ref, row_ref, out_ref, place_ref, v_ref, vs_ref, beam_ref, sems):
    copies = fetch_volts(volt_ref, v_ref, sems)
    for copy in copies:
        copy.start()
    mark_places(slot_ref, place_ref)
    outs = []
    for gy in range(2):
        copies[gy * 2].wait()
        copies[gy * 2 + 1].wait()

        def store(pol, row, lane, value, gy=gy):
            beam_ref[gy, pol, row : row + NS, lane : lane + LANES] = value

        form_beams(v_ref[gy].reshape(FEEDS, 2 * LANES), row_ref, place_ref, vs_ref, store)
        outs.append(pltpu.make_async_copy(beam_ref.at[gy], out_ref.at[gy], sems.at[4 + gy]))
        outs[gy].start()
    for copy in outs:
        copy.wait()


def early_kernel(volt_ref, slot_ref, row_ref, late_ref, table_ref, out_ref, place_ref, v_ref, vs_ref, beam_ref, sems):
    wide = 2 * LANES
    copies = fetch_volts(volt_ref, v_ref, sems)
    for gy in range(2):
        copies.append(
            pltpu.make_async_copy(
                late_ref.at[gy], beam_ref.at[:, :, pl.ds((gy * 2 + 1) * wide, wide)], sems.at[4 + gy]
            )
        )
    for copy in copies[:2]:
        copy.start()
    mark_places(slot_ref, place_ref)
    for gy in range(2):
        copies[gy * 2].wait()
        copies[gy * 2 + 1].wait()
        if gy == 0:
            for copy in copies[2:]:
                copy.start()

        def store(pol, row, lane, value, gy=gy):
            at = gy * 2 * wide + lane
            beam_ref[pol, row : row + NS, at : at + LANES] = value

        form_beams(v_ref[gy].reshape(FEEDS, wide), row_ref, place_ref, vs_ref, store)
        copies[4 + gy].wait()
        for n in range(gy * 2, gy * 2 + 2):
            for at in range(0, BEAMS, NS):
                total = None
                for pol in range(POLS):
                    bands = jnp.dot(
                        beam_ref[pol, at : at + NS, : (n + 1) * wide],
                        table_ref[(3 - n) * wide :, :],
                        preferred_element_type=jnp.float32,
                    )
                    power = bands * bands
                    total = power if total is None else total + power
                value = (total[:, :LANES] + total[:, LANES:]) * (1.0 / UP)
                out_ref[at // 16 : at // 16 + NS // 16, gy, n % 2] = value.reshape(NS // 16, 16, LANES).astype(
                    jnp.bfloat16
                )


def back(volt, slots, rows, *more):
    whole = pl.BlockSpec(memory_space=pltpu.VMEM)
    there = pl.BlockSpec(memory_space=pl.ANY)
    far = pl.BlockSpec(memory_space=pltpu.HBM)
    scratch = [
        pltpu.VMEM((FEEDS, FEEDS), jnp.bfloat16),
        pltpu.VMEM((2, PEERS // 2, FLOC, 2 * LANES), jnp.bfloat16),
        pltpu.VMEM((FEEDS, 2 * LANES), jnp.bfloat16),
    ]
    if more:
        kernel, specs, name = early_kernel, [there, whole, whole, far, whole], "back_early"
        shape, out = (BEAMS // 16, 2, 2, 16, LANES), whole
        scratch += [pltpu.VMEM((POLS, BEAMS, 4 * 2 * LANES), jnp.bfloat16), pltpu.SemaphoreType.DMA((6,))]
    else:
        kernel, specs, name = late_kernel, [there, whole, whole], "back_late"
        shape, out = (SPARE, POLS, BEAMS, 2 * LANES), far
        scratch += [pltpu.VMEM((2, POLS, BEAMS, 2 * LANES), jnp.bfloat16), pltpu.SemaphoreType.DMA((6,))]
    return pl.pallas_call(
        kernel,
        in_specs=specs,
        out_specs=out,
        out_shape=jax.ShapeDtypeStruct(shape, jnp.bfloat16),
        scratch_shapes=scratch,
        compiler_params=pltpu.CompilerParams(vmem_limit_bytes=(48 if more else 40) * MIB),
        cost_estimate=pl.CostEstimate(flops=6 << 30, bytes_accessed=6 << 20, transcendentals=0),
        name=name,
    )(volt.reshape(PEERS // 2, 2, 2, FLOC, LANES), slots, rows, *more)


def body(raw_samples, delays, grid_slot):
    rim = raw_samples[:, raw_samples.shape[1] - (PTAPS - 1) * NFFT :]
    halo = lax.ppermute(rim, "gy", [(0, 1)])
    weights = jnp.asarray(taper(PTAPS, NFFT))
    table = jnp.asarray(dft_table())
    rows = jnp.asarray(row_table())
    slots = grid_slot.reshape(1, FEEDS)
    me = lax.axis_index(BOTH)
    sub = lax.dynamic_slice_in_dim(jnp.asarray(sub_table()), PPG - me % PPG, PPG, axis=2)
    sub = sub.reshape(UTAPS * 2 * LANES, 2 * LANES)

    late = front(True, raw_samples, rim, delays, weights, table)
    late, halo = lax.optimization_barrier((late, halo))
    late = lax.all_to_all(late, BOTH, 0, 0, tiled=True)
    early = front(False, raw_samples, halo, delays, weights, table)
    early, late = lax.optimization_barrier((early, late))
    early = lax.all_to_all(early, BOTH, 0, 0, tiled=True)
    beams = back(late, slots, rows)
    intens = back(early, slots, rows, beams, sub).reshape(PEERS, 2, 16, LANES)
    intens = lax.all_to_all(intens, BOTH, 0, 0, tiled=True)
    return jnp.transpose(intens, (2, 1, 0, 3)).reshape(16, 2, CHAN * UP)


def solution(mesh):
    return jax.shard_map(
        body,
        mesh=mesh,
        in_specs=(P("gx", "gy"), P("gx"), P()),
        out_specs=P("gx", "gy", None),
        check_vma=False,
    )
```

```python
import functools
import math

import jax
import jax.numpy as jnp
import ml_dtypes
import numpy as np
from jax import lax
from jax.experimental import pallas as pl
from jax.experimental.pallas import tpu as pltpu
from jax.sharding import PartitionSpec as P

CHAN = 1024
EW = 4
NS = 256
UP = 16
POLS = 2
PTAPS = 4
UTAPS = 4
NFFT = 2048
NSPAD = 512
BEAMS = 1024
FEEDS = 2048

LANES = 128
PEERS = 128
CPD = CHAN // PEERS
PPG = 2 * LANES // CPD
SPANS = CHAN // (2 * LANES)
FLOC = 32
HALF = 16
BOTH = ("gx", "gy")
MIB = 1024 * 1024
SPARE = 16


def taper(tap_count, seg_length):
    total_len = tap_count * seg_length
    places = np.arange(total_len, dtype=np.float64)
    centre = (places - 0.5 * total_len + 0.5) / seg_length
    hann_part = 0.5 - 0.5 * np.cos(2.0 * math.pi * (places + 0.5) / total_len)
    return (np.sinc(centre) * hann_part).reshape(tap_count, seg_length).astype(np.float32)


def dft_table():
    rows = np.arange(NFFT // 2)
    cols = np.arange(CHAN).reshape(SPANS, LANES, 2).transpose(0, 2, 1)
    phases = (rows[None, None, :, None] * cols[:, :, None, :] % NFFT) * (2.0 * math.pi / NFFT)
    norm_scale = 1.0 / math.sqrt(NFFT)
    both = np.concatenate([np.cos(phases), -np.sin(phases)], axis=3) * norm_scale
    return both.astype(np.float32).astype(ml_dtypes.bfloat16)


def row_table():
    place = np.arange(NS)
    phases = (place[:, None] * place[None, :] % NSPAD) * (2.0 * math.pi / NSPAD)
    norm_scale = 1.0 / math.sqrt(BEAMS)
    both = np.concatenate([np.cos(phases), np.sin(phases)], axis=0) * norm_scale
    return both.astype(np.float32).astype(ml_dtypes.bfloat16)


def sub_table():
    fir = taper(UTAPS, UP)
    q = np.arange(UP)
    phases = (q[:, None] * q[None, :] % UP) * (2.0 * math.pi / UP)
    cosine = fir[:, :, None] * np.cos(phases).astype(np.float32)[None]
    sine = fir[:, :, None] * np.sin(phases).astype(np.float32)[None]
    table = np.zeros((UTAPS, 2, UP, 2, CPD // 2, 2, CPD, UP), np.float32)
    for k in range(CPD):
        table[:, 0, :, k % 2, k // 2, 0, k, :] = cosine
        table[:, 0, :, k % 2, k // 2, 1, k, :] = -sine
        table[:, 1, :, k % 2, k // 2, 0, k, :] = sine
        table[:, 1, :, k % 2, k // 2, 1, k, :] = cosine
    table = table.reshape(UTAPS, 2, PPG, CPD // 2, 2 * LANES)
    return np.concatenate([table, table], axis=2).astype(ml_dtypes.bfloat16)


def turns(index):
    quarter = (index + NFFT // 8) // (NFFT // 4)
    angle = (index - quarter * (NFFT // 4)).astype(jnp.float32) * (2.0 * math.pi / NFFT)
    sq = angle * angle
    sine = angle * (1.0 + sq * (-1.0 / 6 + sq * (1.0 / 120 + sq * (-1.0 / 5040 + sq * (1.0 / 362880)))))
    cosine = 1.0 + sq * (-1.0 / 2 + sq * (1.0 / 24 + sq * (-1.0 / 720 + sq * (1.0 / 40320 - sq * (1.0 / 3628800)))))
    odd = quarter % 2 == 1
    first, second = jnp.where(odd, -sine, cosine), jnp.where(odd, cosine, sine)
    back = (quarter // 2) % 2 == 1
    return jnp.where(back, -first, first), jnp.where(back, -second, second)


def front_kernel(late, raw_ref, halo_ref, delay_ref, w_ref, tab_ref, out_ref, *scratch):
    ext_ref, x_ref, t_ref, o_ref, cos_ref, sin_ref, raw_sems, tab_sems, out_sems = scratch
    lead = (PTAPS - 1) * NFFT
    copies = []
    for h in range(2):
        rows = pl.ds(h * 16, 16)
        if late:
            pairs = [(raw_ref.at[rows, pl.ds(HALF * NFFT - lead, HALF * NFFT + lead)], ext_ref.at[rows, :])]
        else:
            pairs = [
                (raw_ref.at[rows, pl.ds(0, HALF * NFFT)], ext_ref.at[rows, pl.ds(lead, HALF * NFFT)]),
                (halo_ref.at[rows, :], ext_ref.at[rows, pl.ds(0, lead)]),
            ]
        copies.append([pltpu.make_async_copy(src, dst, raw_sems.at[h, i]) for i, (src, dst) in enumerate(pairs)])
    tables = [pltpu.make_async_copy(tab_ref.at[s], t_ref.at[s], tab_sems.at[s]) for s in range(SPANS)]
    for copy in copies[0] + copies[1]:
        copy.start()

    sub = lax.broadcasted_iota(jnp.int32, (8, LANES), 0)
    lane = lax.broadcasted_iota(jnp.int32, (8, LANES), 1)
    for g in range(FLOC // 8):
        delay = jnp.zeros((8, LANES), jnp.int32)
        for i in range(8):
            delay = jnp.where(sub == i, delay_ref[g * 8 + i], delay)
        for s in range(SPANS):
            for odd in range(2):
                cosine, sine = turns((delay * (2 * LANES * s + odd + 2 * lane)) % NFFT)
                cos_ref[s * 2 + odd, g * 8 : g * 8 + 8, :] = cosine
                sin_ref[s * 2 + odd, g * 8 : g * 8 + 8, :] = sine

    def tile(h, step, carry):
        at = pl.multiple_of(step * LANES, LANES)
        half = NFFT // 2
        rows = slice(h * 16, h * 16 + 16)
        totals = []
        for side in range(2):
            weights = [w_ref[p : p + 1, pl.ds(at + side * half, LANES)] for p in range(PTAPS)]
            frames = [
                ext_ref[rows, pl.ds(pl.multiple_of(at + side * half + m * NFFT, LANES), LANES)].astype(jnp.float32)
                for m in range(HALF + PTAPS - 1)
            ]
            sums = []
            for m in range(HALF):
                total = frames[m] * weights[0]
                for p in range(1, PTAPS):
                    total = total + frames[m + p] * weights[p]
                sums.append(total)
            totals.append(sums)
        for m in range(HALF):
            place = pl.ds(h * 256 + m * 16, 16)
            x_ref[0, place, pl.ds(at, LANES)] = (totals[0][m] + totals[1][m]).astype(jnp.bfloat16)
            x_ref[1, place, pl.ds(at, LANES)] = (totals[0][m] - totals[1][m]).astype(jnp.bfloat16)
        return carry

    for h in range(2):
        for copy in copies[h]:
            copy.wait()
        if h == 0:
            for copy in tables:
                copy.start()
        lax.fori_loop(0, NFFT // 2 // LANES, functools.partial(tile, h), 0)

    block = lax.broadcasted_iota(jnp.int32, (16, LANES), 1) // (LANES // PPG)
    bits = [(block // (1 << t)) % 2 == 1 for t in range(5)]
    outs = []
    for s in range(SPANS):
        tables[s].wait()
        spectra = [jnp.dot(x_ref[odd], t_ref[s, odd], preferred_element_type=jnp.float32) for odd in range(2)]
        for h in range(2):
            rows = slice(h * 16, h * 16 + 16)
            parts = [[None] * PPG, [None] * PPG]
            for odd in range(2):
                cosine, sine = cos_ref[s * 2 + odd, rows, :], sin_ref[s * 2 + odd, rows, :]
                for m in range(HALF):
                    i = m * 2 + odd
                    row = h * 256 + m * 16
                    real = spectra[odd][row : row + 16, :LANES]
                    imag = spectra[odd][row : row + 16, LANES:]
                    turned = (real * cosine + imag * sine, imag * cosine - real * sine)
                    for x in range(2):
                        value = pltpu.roll(turned[x], i * (LANES // PPG), 1) if i else turned[x]
                        parts[x][i] = value.astype(jnp.bfloat16)
            for x in range(2):
                held = parts[x]
                for t in range(5):
                    held = [jnp.where(bits[t], held[(i + (1 << t)) % PPG], held[i]) for i in range(PPG)]
                for p in range(PPG):
                    o_ref[s, p, x, rows, :] = held[(PPG - p) % PPG]
        copy = pltpu.make_async_copy(o_ref.at[s], out_ref.at[pl.ds(s * PPG, PPG)], out_sems.at[s])
        copy.start()
        outs.append(copy)
    for copy in outs:
        copy.wait()


def front(late, raw, halo, delays, weights, table):
    wide = (HALF + PTAPS - 1) * NFFT
    there = pl.BlockSpec(memory_space=pl.ANY)
    return pl.pallas_call(
        functools.partial(front_kernel, late),
        in_specs=[
            pl.BlockSpec(memory_space=pltpu.HBM),
            there,
            pl.BlockSpec(memory_space=pltpu.SMEM),
            pl.BlockSpec(memory_space=pltpu.VMEM),
            pl.BlockSpec(memory_space=pltpu.HBM),
        ],
        out_specs=there,
        out_shape=jax.ShapeDtypeStruct((PEERS, 2, FLOC, LANES), jnp.bfloat16),
        scratch_shapes=[
            pltpu.VMEM((FLOC, wide), jnp.bfloat16),
            pltpu.VMEM((2, FLOC * HALF, NFFT // 2), jnp.bfloat16),
            pltpu.VMEM((SPANS, 2, NFFT // 2, 2 * LANES), jnp.bfloat16),
            pltpu.VMEM((SPANS, PPG, 2, FLOC, LANES), jnp.bfloat16),
            pltpu.VMEM((2 * SPANS, FLOC, LANES), jnp.float32),
            pltpu.VMEM((2 * SPANS, FLOC, LANES), jnp.float32),
            pltpu.SemaphoreType.DMA((2, 2)),
            pltpu.SemaphoreType.DMA((SPANS,)),
            pltpu.SemaphoreType.DMA((SPANS,)),
        ],
        compiler_params=pltpu.CompilerParams(vmem_limit_bytes=(58 if late else 30) * MIB),
        cost_estimate=pl.CostEstimate(flops=2 * 512 * 1024 * 2048, bytes_accessed=9 << 20, transcendentals=0),
        name="front_late" if late else "front_early",
    )(raw, halo, delays, weights, table)


def fetch_volts(volt_ref, v_ref, sems):
    return [
        pltpu.make_async_copy(
            volt_ref.at[:, gy, x], v_ref.at[gy, :, :, pl.ds(x * LANES, LANES)], sems.at[gy * 2 + x]
        )
        for gy in range(2)
        for x in range(2)
    ]


def mark_places(slot_ref, place_ref, pol):
    slots = slot_ref[...]
    for r in range(pol * EW, pol * EW + EW):
        row = lax.broadcasted_iota(jnp.int32, (NS, FEEDS), 0) + r * NS
        place_ref[r * NS : (r + 1) * NS, :] = jnp.where(row == slots, 1.0, 0.0).astype(jnp.bfloat16)


def form_beams(volts, row_ref, place_ref, vs_ref, store):
    for at in range(0, FEEDS, BEAMS):
        placed = jnp.dot(place_ref[at : at + BEAMS, :], volts, preferred_element_type=jnp.float32)
        vs_ref[at : at + BEAMS, :] = placed.astype(jnp.bfloat16)
    for pol in range(POLS):
        parts = []
        for c in range(EW):
            at = (pol * EW + c) * NS
            both = jnp.dot(row_ref[...], vs_ref[at : at + NS, :], preferred_element_type=jnp.float32)
            cosine, sine = both[:NS], both[NS:]
            parts.append((cosine[:, :LANES] - sine[:, LANES:], cosine[:, LANES:] + sine[:, :LANES]))
        (r0, i0), (r1, i1), (r2, i2), (r3, i3) = parts
        ar, ai, br, bi = r0 + r2, i0 + i2, r0 - r2, i0 - i2
        cr, ci, dr, di = r1 + r3, i1 + i3, r1 - r3, i1 - i3
        formed = [(ar + cr, ai + ci), (br - di, bi + dr), (ar - cr, ai - ci), (br + di, bi - dr)]
        for e in range(EW):
            for x in range(2):
                store(pol, e * NS, x * LANES, formed[e][x].astype(jnp.bfloat16))


def late_kernel(volt_ref, slot_ref, row_ref, out_ref, place_ref, v_ref, vs_ref, beam_ref, sems):
    copies = fetch_volts(volt_ref, v_ref, sems)
    for copy in copies:
        copy.start()
    mark_places(slot_ref, place_ref, 0)
    outs = []
    for gy in range(2):
        copies[gy * 2].wait()
        copies[gy * 2 + 1].wait()
        if gy == 0:
            mark_places(slot_ref, place_ref, 1)

        def store(pol, row, lane, value, gy=gy):
            beam_ref[gy, pol, row : row + NS, lane : lane + LANES] = value

        form_beams(v_ref[gy].reshape(FEEDS, 2 * LANES), row_ref, place_ref, vs_ref, store)
        outs.append(pltpu.make_async_copy(beam_ref.at[gy], out_ref.at[gy], sems.at[4 + gy]))
        outs[gy].start()
    for copy in outs:
        copy.wait()


def early_kernel(volt_ref, slot_ref, row_ref, late_ref, table_ref, out_ref, place_ref, v_ref, vs_ref, beam_ref, sems):
    wide = 2 * LANES
    copies = fetch_volts(volt_ref, v_ref, sems)
    for gy in range(2):
        copies.append(
            pltpu.make_async_copy(
                late_ref.at[gy], beam_ref.at[:, :, pl.ds((gy * 2 + 1) * wide, wide)], sems.at[4 + gy]
            )
        )
    for copy in copies[:2]:
        copy.start()
    mark_places(slot_ref, place_ref, 0)
    for gy in range(2):
        copies[gy * 2].wait()
        copies[gy * 2 + 1].wait()
        if gy == 0:
            for copy in copies[2:]:
                copy.start()
            mark_places(slot_ref, place_ref, 1)

        def store(pol, row, lane, value, gy=gy):
            at = gy * 2 * wide + lane
            beam_ref[pol, row : row + NS, at : at + LANES] = value

        form_beams(v_ref[gy].reshape(FEEDS, wide), row_ref, place_ref, vs_ref, store)
        copies[4 + gy].wait()
        for n in range(gy * 2, gy * 2 + 2):
            for at in range(0, BEAMS, NS):
                total = None
                for pol in range(POLS):
                    bands = jnp.dot(
                        beam_ref[pol, at : at + NS, : (n + 1) * wide],
                        table_ref[(3 - n) * wide :, :],
                        preferred_element_type=jnp.float32,
                    )
                    power = bands * bands
                    total = power if total is None else total + power
                value = (total[:, :LANES] + total[:, LANES:]) * (1.0 / UP)
                out_ref[at // 16 : at // 16 + NS // 16, gy, n % 2] = value.reshape(NS // 16, 16, LANES).astype(
                    jnp.bfloat16
                )


def back(volt, slots, rows, *more):
    whole = pl.BlockSpec(memory_space=pltpu.VMEM)
    there = pl.BlockSpec(memory_space=pl.ANY)
    far = pl.BlockSpec(memory_space=pltpu.HBM)
    scratch = [
        pltpu.VMEM((FEEDS, FEEDS), jnp.bfloat16),
        pltpu.VMEM((2, PEERS // 2, FLOC, 2 * LANES), jnp.bfloat16),
        pltpu.VMEM((FEEDS, 2 * LANES), jnp.bfloat16),
    ]
    if more:
        kernel, specs, name = early_kernel, [there, whole, whole, far, whole], "back_early"
        shape, out = (BEAMS // 16, 2, 2, 16, LANES), whole
        scratch += [pltpu.VMEM((POLS, BEAMS, 4 * 2 * LANES), jnp.bfloat16), pltpu.SemaphoreType.DMA((6,))]
    else:
        kernel, specs, name = late_kernel, [there, whole, whole], "back_late"
        shape, out = (SPARE, POLS, BEAMS, 2 * LANES), far
        scratch += [pltpu.VMEM((2, POLS, BEAMS, 2 * LANES), jnp.bfloat16), pltpu.SemaphoreType.DMA((6,))]
    return pl.pallas_call(
        kernel,
        in_specs=specs,
        out_specs=out,
        out_shape=jax.ShapeDtypeStruct(shape, jnp.bfloat16),
        scratch_shapes=scratch,
        compiler_params=pltpu.CompilerParams(vmem_limit_bytes=(48 if more else 40) * MIB),
        cost_estimate=pl.CostEstimate(flops=6 << 30, bytes_accessed=6 << 20, transcendentals=0),
        name=name,
    )(volt.reshape(PEERS // 2, 2, 2, FLOC, LANES), slots, rows, *more)


def body(raw_samples, delays, grid_slot):
    rim = raw_samples[:, raw_samples.shape[1] - (PTAPS - 1) * NFFT :]
    halo = lax.ppermute(rim, "gy", [(0, 1)])
    weights = jnp.asarray(taper(PTAPS, NFFT))
    table = jnp.asarray(dft_table())
    rows = jnp.asarray(row_table())
    slots = grid_slot.reshape(1, FEEDS)
    me = lax.axis_index(BOTH)
    sub = lax.dynamic_slice_in_dim(jnp.asarray(sub_table()), PPG - me % PPG, PPG, axis=2)
    sub = sub.reshape(UTAPS * 2 * LANES, 2 * LANES)

    late = front(True, raw_samples, rim, delays, weights, table)
    late, halo = lax.optimization_barrier((late, halo))
    late = lax.all_to_all(late, BOTH, 0, 0, tiled=True)
    early = front(False, raw_samples, halo, delays, weights, table)
    early, late = lax.optimization_barrier((early, late))
    early = lax.all_to_all(early, BOTH, 0, 0, tiled=True)
    beams = back(late, slots, rows)
    intens = back(early, slots, rows, beams, sub).reshape(PEERS, 2, 16, LANES)
    intens = lax.all_to_all(intens, BOTH, 0, 0, tiled=True)
    return jnp.transpose(intens, (2, 1, 0, 3)).reshape(16, 2, CHAN * UP)


def solution(mesh):
    return jax.shard_map(
        body,
        mesh=mesh,
        in_specs=(P("gx", "gy"), P("gx"), P()),
        out_specs=P("gx", "gy", None),
        check_vma=False,
    )
```
